32 devices in a mesh: energy: 16 (over z, y, x), slab: 2 (over core).
Axes of the slice: x: 2, y: 2, z: 4, core: 2. Of those that a mesh axis runs over, the one named last changes fastest.
Arguments:
- retarded: bfloat16 [16, 4, 5, 2, 384, 384], P('energy', 'slab'), may hold values from -0.09375 to 0.09375
- ballistic: float32 [16, 4, 2, 384, 384], P('energy', 'slab'), may hold values from -6 to 6
- coupling: bfloat16 [2, 384, 384], replicated, may hold values from -0.3125 to 0.3125
- occupation: float32 [2], replicated, may hold values from 0.2 to 2
- shifts: int32 [2], replicated, may hold values from 1 to 2, as said below
Outputs:
- lesser: float32 [16, 4, 2, 384, 384], P('energy', 'slab')
The draws below stay inside these ranges and needn't reach their ends.
Inputs may be any that keep to these rules, and one draw needn't show every extreme that they name: The modes' shifts are the numbers 1 to 2 in some order.
All inputs are finite; a program needn't handle non-finite values.
Results may differ from the reference program's by a relative error of at most 0.012.
Values may be sent and summed in bfloat16 or wider, within the bound.
A program may use at most 128 MiB of HBM per device.

```python
import math
import jax
import jax.numpy as jnp
from jax import lax

B = 384
MODES = 2
ITERS = 2
NE = 16
NBLK = 4


def draw_shifts(key, part):
    return jax.random.permutation(jax.random.fold_in(key, 17), jnp.arange(1, MODES + 1, dtype=jnp.int32)).astype(jnp.int32)


def level_of(own_key, shape, cuts, smallest, top_value):
    def one(axis_at, shards_of):
        steps = jax.random.uniform(jax.random.fold_in(jax.random.fold_in(own_key, 6), axis_at), (shards_of,), jnp.float32, smallest / len(cuts), top_value / len(cuts))
        return jnp.repeat(jnp.exp(steps), shape[axis_at] // shards_of).reshape((-1,) + (1,) * (len(shape) - axis_at - 1))

    loudness = one(*cuts[0])
    for cut in cuts[1:]:
        loudness = loudness * one(*cut)
    return loudness


def noise(own_key, shape, deviation, limit, cuts=(), kind=jnp.bfloat16):
    loudness = level_of(own_key, shape, cuts, -0.22, 0.18) if cuts else 1.0
    values = jax.random.normal(own_key, shape, jnp.float32) * deviation * loudness
    return jnp.minimum(jnp.maximum(values, -limit), limit).astype(kind)


def setup_inputs(seed: int = 0) -> dict:
    splits = jax.random.split(jax.random.key(seed), 6)
    return {
        "retarded": noise(splits[0], (NE, NBLK, 5, 2, B, B), (10 * B) ** -0.5, 0.09375, ((0, 16), (1, 2))),
        "ballistic": noise(splits[1], (NE, NBLK, 2, B, B), 1.0, 6.0, ((0, 16), (1, 2)), jnp.float32),
        "coupling": noise(splits[2], (MODES, B, B), B ** -0.5, 0.3125),
        "occupation": jnp.clip(jnp.exp(jax.random.uniform(splits[3], (MODES,), jnp.float32, math.log(0.2), math.log(2.0))), 0.2, 2.0),
        "shifts": draw_shifts(jax.random.fold_in(splits[5], 71), 0),
    }


def reference(retarded, ballistic, coupling, occupation, shifts):
    energies = ballistic.shape[0]
    blocks = ballistic.shape[1]
    highest = lax.Precision.HIGHEST
    weights = coupling.astype(jnp.float32)
    current = ballistic
    for iteration in range(ITERS):
        rounded = lax.optimization_barrier(current.astype(jnp.bfloat16)).astype(jnp.float32)
        padded = jnp.pad(rounded, ((MODES, MODES), (0, 0), (0, 0), (0, 0), (0, 0)))
        scatter_total = jnp.zeros_like(current)
        for mode in range(MODES):
            rising = lax.dynamic_slice_in_dim(padded, (MODES + shifts[mode]).astype(jnp.int32), energies, 0)
            falling = lax.dynamic_slice_in_dim(padded, (MODES - shifts[mode]).astype(jnp.int32), energies, 0)
            mixture = (1.0 + occupation[mode]) * rising + occupation[mode] * falling
            mixture = lax.optimization_barrier(mixture.astype(jnp.bfloat16)).astype(jnp.float32)
            inner = jnp.einsum('ab,enrbc->enrac', weights[mode], mixture, precision=highest)
            inner = lax.optimization_barrier(inner.astype(jnp.bfloat16)).astype(jnp.float32)
            scatter_total = scatter_total + jnp.einsum('enrab,cb->enrac', inner, weights[mode], precision=highest)
        scatter_round = lax.optimization_barrier(scatter_total.astype(jnp.bfloat16)).astype(jnp.float32)
        scatter_pad = jnp.pad(scatter_round, ((0, 0), (2, 2), (0, 0), (0, 0), (0, 0)))

        def one_energy(items):
            band, around, source = items
            band = band.astype(jnp.float32)
            nearby = jnp.stack([around[offset:offset + blocks] for offset in range(5)], axis=1)
            ret_real = band[:, :, 0]
            ret_imag = band[:, :, 1]
            near_real = nearby[:, :, 0]
            near_imag = nearby[:, :, 1]
            pattern = 'njab,njbc->njac'
            left_real = jnp.einsum(pattern, ret_real, near_real, precision=highest) - jnp.einsum(pattern, ret_imag, near_imag, precision=highest)
            left_imag = jnp.einsum(pattern, ret_real, near_imag, precision=highest) + jnp.einsum(pattern, ret_imag, near_real, precision=highest)
            left_real = lax.optimization_barrier(left_real.astype(jnp.bfloat16)).astype(jnp.float32)
            left_imag = lax.optimization_barrier(left_imag.astype(jnp.bfloat16)).astype(jnp.float32)
            closing = 'njab,njcb->nac'
            out_real = jnp.einsum(closing, left_real, ret_real, precision=highest) + jnp.einsum(closing, left_imag, ret_imag, precision=highest)
            out_imag = jnp.einsum(closing, left_imag, ret_real, precision=highest) - jnp.einsum(closing, left_real, ret_imag, precision=highest)
            return source + jnp.stack([out_real, out_imag], axis=1)

        current = lax.map(one_energy, (retarded, scatter_pad, ballistic))
    return current
```

```python
import functools

import jax
import jax.numpy as jnp
from jax import lax
from jax.experimental import pallas as pl
from jax.experimental.pallas import tpu as pltpu
from jax.sharding import PartitionSpec as P

ITERS = 2
ROWS = 64
MESH = pl.DeviceIdType.MESH

PAIRS = ((0, 0), (1, 0), (0, 1), (1, 1), (0, 2), (0, 3), (1, 2))


def dot(a, b):
    return jnp.dot(a, b, preferred_element_type=jnp.float32)


def dot_nt(a, b):
    return lax.dot_general(a, b, (((1,), (1,)), ((), ())), preferred_element_type=jnp.float32)


def kernel(
    size, retarded, ballistic, coupling, occupation, shifts, lesser,
    base, total, own, near, far, mix_out, mix_in, mode2, band, wide, half, left, pair_c,
    base_sem, band_sem, own_send, relay_send, mix_send, wide_send,
    near_recv, far_recv, mix_recv, wide_recv, out_sem, energies,
):
    width = 2 * size
    per_block = size // ROWS
    steps = 2 * per_block
    tile = 256 if width % 256 == 0 else 128
    e = lax.axis_index("energy")
    s = lax.axis_index("slab")
    xb = e % 2
    yb = (e // 2) % 2
    d = 1 - 2 * yb
    near_dev = (e + 2 * d, s)
    relay_dev = (e + 4 * d, s)
    far_dev = (e - 4 * d, s)
    mate_dev = (e + 1 - 2 * xb, s)
    slab_dev = (e, 1 - s)
    has_relay = jnp.logical_and(e + 4 * d >= 0, e + 4 * d < energies)
    has_far = jnp.logical_and(e - 4 * d >= 0, e - 4 * d < energies)

    def block_at(slot):
        return (1 - slot) * (1 - 2 * s) + s

    def offset_at(slot, source):
        here = 2 * s + block_at(slot)
        if source % 2 == 0:
            there = 2 * s + block_at(source // 2)
        else:
            a = 1 - source // 2
            there = 2 * (1 - s) + a * (2 * s - 1) + 1 - s
        return there - here + 2

    def base_copy(slot, part):
        return pltpu.make_async_copy(
            ballistic.at[0, block_at(slot), part],
            base.at[pl.ds(slot * size, size), pl.ds(part * size, size)],
            base_sem.at[slot, part],
        )

    def band_copy(p, k):
        slot, source = PAIRS[p]
        part = (0, 1, 0)[k]
        row, col = ((0, 0), (0, 1), (1, 1))[k]
        return pltpu.make_async_copy(
            retarded.at[0, block_at(slot), offset_at(slot, source), part],
            band.at[p, pl.ds(row * size, size), pl.ds(col * size, size)],
            band_sem.at[p, k],
        )

    def rows_of(c):
        return pl.ds(pl.multiple_of(c * ROWS, ROWS), ROWS)

    def remote(src, dst, send, recv, device):
        return pltpu.make_async_remote_copy(
            src_ref=src, dst_ref=dst, send_sem=send, recv_sem=recv,
            device_id=device, device_id_type=MESH,
        )

    def own_copy(t, c):
        return remote(
            own.at[t, rows_of(c)], near.at[t, rows_of(c)],
            own_send.at[t, c], near_recv.at[t, c], near_dev,
        )

    def relay_copy(t, c):
        return remote(
            near.at[t, rows_of(c)], far.at[t, rows_of(c)],
            relay_send.at[t, c], far_recv.at[t, c], relay_dev,
        )

    def mix_copy(t, c):
        return remote(
            mix_out.at[t, rows_of(c)], mix_in.at[t, rows_of(c)],
            mix_send.at[t, c], mix_recv.at[t, c], mate_dev,
        )

    def wide_copy(t, slot):
        return remote(
            wide.at[t, 2 * slot, pl.ds(0, size)], wide.at[t, 2 * slot + 1, pl.ds(0, size)],
            wide_send.at[t, slot], wide_recv.at[t, slot], slab_dev,
        )

    for slot in range(2):
        for part in range(2):
            base_copy(slot, part).start()

    barrier = pltpu.get_barrier_semaphore()
    for device in (near_dev, mate_dev, slab_dev):
        pl.semaphore_signal(barrier, inc=1, device_id=device, device_id_type=MESH)

    @pl.when(has_relay)
    def _():
        pl.semaphore_signal(barrier, inc=1, device_id=relay_dev, device_id_type=MESH)

    @pl.when(has_far)
    def _():
        pl.semaphore_signal(barrier, inc=1, device_id=far_dev, device_id_type=MESH)

    for p in range(len(PAIRS)):
        for k in range(3):
            band_copy(p, k).start()

    first = (shifts[0] == 1)
    occ1 = jnp.where(first, occupation[0], occupation[1])
    occ2 = jnp.where(first, occupation[1], occupation[0])
    pick = jnp.where(first, 0, 1)
    pair_c[:, :size] = coupling[pick]
    pair_c[:, size:] = coupling[1 - pick]

    @pl.when(jnp.logical_not(has_far))
    def _():
        far[...] = jnp.zeros_like(far)

    own_weight = jnp.where(xb == 0, occ1, 1.0 + occ1)
    other_weight = jnp.where(xb == 0, 1.0 + occ1, occ1)
    near_weight = jnp.where(yb == 0, 1.0 + occ2, occ2)
    far_weight = jnp.where(yb == 0, occ2, 1.0 + occ2)

    for slot in range(2):
        for part in range(2):
            base_copy(slot, part).wait()
        rows = pl.ds(slot * size, size)
        own[0, rows] = base[rows].astype(jnp.bfloat16)
        if slot == 0:
            peers = 3 + has_relay.astype(jnp.int32) + has_far.astype(jnp.int32)
            pl.semaphore_wait(barrier, peers)

        @pl.loop(slot * per_block, (slot + 1) * per_block)
        def _(c):
            own_copy(0, c).start()

    for p in range(len(PAIRS)):
        for k in range(3):
            band_copy(p, k).wait()
        band[p, pl.ds(size, size), pl.ds(0, size)] = -band[p, pl.ds(0, size), pl.ds(size, size)]

    def send_mixture(t, c, other):
        rows = rows_of(c)
        mixed = own_weight * own[t, rows].astype(jnp.float32)
        mixed = mixed + other_weight * other[t, rows].astype(jnp.float32)
        mix_out[t, rows] = mixed.astype(jnp.bfloat16)
        mix_copy(t, c).start()

    def near_step(t, c):
        own_copy(t, c).wait_recv()

        @pl.when(has_relay)
        def _():
            relay_copy(t, c).start()

        @pl.when(xb == yb)
        def _():
            send_mixture(t, c, near)

    def far_step(t, c):
        @pl.when(has_far)
        def _():
            relay_copy(t, c).wait_recv()

        @pl.when(xb != yb)
        def _():
            send_mixture(t, c, far)

        rows = rows_of(c)
        mixed = near_weight * near[t, rows].astype(jnp.float32)
        mixed = mixed + far_weight * far[t, rows].astype(jnp.float32)
        mode2[rows] = mixed.astype(jnp.bfloat16)

    def step(t, c):
        near_step(t, c)
        far_step(t, c - 1)

    def widen(t, source):
        wide[t, source, size:, :size] = -wide[t, source, :size, size:]
        wide[t, source, size:, size:] = wide[t, source, :size, :size]

    def scatter(t, slot):
        @pl.loop(slot * per_block, (slot + 1) * per_block)
        def _(c):
            mix_copy(t, c).wait_recv()

        rows = pl.ds(slot * size, size)
        for part in range(2):
            cols = pl.ds(part * size, size)
            half[:size, cols] = dot_nt(mix_in[t, rows, cols], pair_c[:, :size]).astype(jnp.bfloat16)
            half[size:, cols] = dot_nt(mode2[rows, cols], pair_c[:, size:]).astype(jnp.bfloat16)

        @pl.loop(0, width // tile)
        def _(n):
            cols = pl.ds(pl.multiple_of(n * tile, tile), tile)
            wide[t, 2 * slot, :size, cols] = dot(pair_c[...], half[:, cols]).astype(jnp.bfloat16)

        wide_copy(t, slot).start()
        widen(t, 2 * slot)

    def receive(t, slot):
        wide_copy(t, slot).wait_recv()
        widen(t, 2 * slot + 1)

    def pair(t, p):
        slot, source = PAIRS[p]
        rows = pl.ds(slot * size, size)
        start = base if p < 2 else total

        @pl.loop(0, width // tile)
        def _(n):
            cols = pl.ds(pl.multiple_of(n * tile, tile), tile)
            left[:, cols] = dot(band[p, :size], wide[t, source, :, cols]).astype(jnp.bfloat16)

        @pl.loop(0, width // tile)
        def _(n):
            cols = pl.ds(pl.multiple_of(n * tile, tile), tile)
            total[rows, cols] = start[rows, cols] + dot_nt(left[...], band[p, cols])

    def out_copy(slot, part):
        return pltpu.make_async_copy(
            total.at[pl.ds(slot * size, size), pl.ds(part * size, size)],
            lesser.at[0, block_at(slot), part],
            out_sem.at[slot, part],
        )

    def finish(t, slot):
        if t == ITERS - 1:
            for part in range(2):
                out_copy(slot, part).start()
            return

        @pl.loop(slot * per_block, (slot + 1) * per_block)
        def _(c):
            own[t + 1, rows_of(c)] = total[rows_of(c)].astype(jnp.bfloat16)
            own_copy(t + 1, c).start()

    for t in range(ITERS):
        near_step(t, 0)
        lag = min(per_block + 3, steps)

        @pl.loop(1, lag)
        def _(c):
            step(t, c)

        scatter(t, 0)
        for p in range(4):
            if lag + p < steps:
                step(t, lag + p)
            if p == 2:
                receive(t, 0)
            pair(t, p)
        if lag + 4 < steps:
            @pl.loop(lag + 4, steps)
            def _(c):
                step(t, c)
        far_step(t, steps - 1)
        scatter(t, 1)
        pair(t, 4)
        receive(t, 1)
        pair(t, 5)
        finish(t, 0)
        pair(t, 6)
        finish(t, 1)

    for slot in range(2):
        for part in range(2):
            out_copy(slot, part).wait()
    for t in range(ITERS):
        for slot in range(2):
            wide_copy(t, slot).wait_send()

        @pl.loop(0, steps)
        def _(c):
            own_copy(t, c).wait_send()
            mix_copy(t, c).wait_send()

            @pl.when(has_relay)
            def _():
                relay_copy(t, c).wait_send()


def shards(energies, retarded, ballistic, coupling, occupation, shifts):
    count, blocks, _, size, _ = ballistic.shape
    assert count == 1 and blocks == 2 and energies % 4 == 0
    assert lax.axis_size("slab") == 2 and size % ROWS == 0
    width = 2 * size
    steps = 2 * size // ROWS
    blob = pltpu.VMEM((ITERS, 2 * size, width), jnp.bfloat16)
    flags = pltpu.SemaphoreType.DMA((ITERS, steps))
    pairs = len(PAIRS)
    flops = 2 * ITERS * (4 * pairs + 8) * width * width * size
    return pl.pallas_call(
        functools.partial(kernel, size, energies=energies),
        out_shape=jax.ShapeDtypeStruct(ballistic.shape, jnp.float32),
        in_specs=[
            pl.BlockSpec(memory_space=pl.ANY),
            pl.BlockSpec(memory_space=pl.ANY),
            pl.BlockSpec(memory_space=pltpu.VMEM),
            pl.BlockSpec(memory_space=pltpu.SMEM),
            pl.BlockSpec(memory_space=pltpu.SMEM),
        ],
        out_specs=pl.BlockSpec(memory_space=pl.ANY),
        scratch_shapes=[
            pltpu.VMEM((2 * size, width), jnp.float32),
            pltpu.VMEM((2 * size, width), jnp.float32),
            blob,
            blob,
            blob,
            blob,
            blob,
            pltpu.VMEM((2 * size, width), jnp.bfloat16),
            pltpu.VMEM((pairs, width, width), jnp.bfloat16),
            pltpu.VMEM((ITERS, 4, width, width), jnp.bfloat16),
            pltpu.VMEM((width, width), jnp.bfloat16),
            pltpu.VMEM((size, width), jnp.bfloat16),
            pltpu.VMEM((size, width), jnp.bfloat16),
            pltpu.SemaphoreType.DMA((2, 2)),
            pltpu.SemaphoreType.DMA((pairs, 3)),
            flags,
            flags,
            flags,
            pltpu.SemaphoreType.DMA((ITERS, 2)),
            flags,
            flags,
            flags,
            pltpu.SemaphoreType.DMA((ITERS, 2)),
            pltpu.SemaphoreType.DMA((2, 2)),
        ],
        cost_estimate=pl.CostEstimate(
            flops=flops, bytes_accessed=retarded.size * 2 + ballistic.size * 8, transcendentals=0
        ),
        compiler_params=pltpu.CompilerParams(
            collective_id=0, has_side_effects=True, vmem_limit_bytes=56 * 1024 * 1024
        ),
    )(retarded, ballistic, coupling, occupation, shifts)


def solution(mesh):
    return jax.shard_map(
        functools.partial(shards, mesh.shape["energy"]),
        mesh=mesh,
        in_specs=(
            P("energy", "slab", None, None, None, None),
            P("energy", "slab", None, None, None),
            P(),
            P(),
            P(),
        ),
        out_specs=P("energy", "slab", None, None, None),
        check_vma=False,
    )
```

```python
import functools

import jax
import jax.numpy as jnp
from jax import lax
from jax.experimental import pallas as pl
from jax.experimental.pallas import tpu as pltpu
from jax.sharding import PartitionSpec as P

ITERS = 2
ROWS = 64
MESH = pl.DeviceIdType.MESH

PAIRS = ((0, 0), (1, 0), (0, 1), (1, 1), (0, 2), (0, 3), (1, 2))


def dot(a, b):
    return jnp.dot(a, b, preferred_element_type=jnp.float32)


def dot_nt(a, b):
    return lax.dot_general(a, b, (((1,), (1,)), ((), ())), preferred_element_type=jnp.float32)


def kernel(
    size, retarded, ballistic, coupling, occupation, shifts, lesser,
    base, total, own, near, far, mix_out, mix_in, mode2, band, wide, half, left, pair_c,
    base_sem, band_sem, own_send, relay_send, mix_send, wide_send,
    near_recv, far_recv, mix_recv, wide_recv, out_sem, energies,
):
    width = 2 * size
    per_block = size // ROWS
    steps = 2 * per_block
    e = lax.axis_index("energy")
    s = lax.axis_index("slab")
    xb = e % 2
    yb = (e // 2) % 2
    d = 1 - 2 * yb
    near_dev = (e + 2 * d, s)
    relay_dev = (e + 4 * d, s)
    far_dev = (e - 4 * d, s)
    mate_dev = (e + 1 - 2 * xb, s)
    slab_dev = (e, 1 - s)
    has_relay = jnp.logical_and(e + 4 * d >= 0, e + 4 * d < energies)
    has_far = jnp.logical_and(e - 4 * d >= 0, e - 4 * d < energies)

    def block_at(slot):
        return (1 - slot) * (1 - 2 * s) + s

    def offset_at(slot, source):
        here = 2 * s + block_at(slot)
        if source % 2 == 0:
            there = 2 * s + block_at(source // 2)
        else:
            a = 1 - source // 2
            there = 2 * (1 - s) + a * (2 * s - 1) + 1 - s
        return there - here + 2

    def base_copy(slot, part):
        return pltpu.make_async_copy(
            ballistic.at[0, block_at(slot), part],
            base.at[pl.ds(slot * size, size), pl.ds(part * size, size)],
            base_sem.at[slot, part],
        )

    def band_copy(p, k):
        slot, source = PAIRS[p]
        part = (0, 1, 0)[k]
        row, col = ((0, 0), (0, 1), (1, 1))[k]
        return pltpu.make_async_copy(
            retarded.at[0, block_at(slot), offset_at(slot, source), part],
            band.at[p, pl.ds(row * size, size), pl.ds(col * size, size)],
            band_sem.at[p, k],
        )

    def rows_of(c):
        return pl.ds(pl.multiple_of(c * ROWS, ROWS), ROWS)

    def remote(src, dst, send, recv, device):
        return pltpu.make_async_remote_copy(
            src_ref=src, dst_ref=dst, send_sem=send, recv_sem=recv,
            device_id=device, device_id_type=MESH,
        )

    def own_copy(t, c):
        return remote(
            own.at[t, rows_of(c)], near.at[t, rows_of(c)],
            own_send.at[t, c], near_recv.at[t, c], near_dev,
        )

    def relay_copy(t, c):
        return remote(
            near.at[t, rows_of(c)], far.at[t, rows_of(c)],
            relay_send.at[t, c], far_recv.at[t, c], relay_dev,
        )

    def mix_copy(t, c):
        return remote(
            mix_out.at[t, rows_of(c)], mix_in.at[t, rows_of(c)],
            mix_send.at[t, c], mix_recv.at[t, c], mate_dev,
        )

    def wide_copy(t, slot):
        return remote(
            wide.at[t, 2 * slot, pl.ds(0, size)], wide.at[t, 2 * slot + 1, pl.ds(0, size)],
            wide_send.at[t, slot], wide_recv.at[t, slot], slab_dev,
        )

    for slot in range(2):
        for part in range(2):
            base_copy(slot, part).start()

    barrier = pltpu.get_barrier_semaphore()
    for device in (near_dev, mate_dev, slab_dev):
        pl.semaphore_signal(barrier, inc=1, device_id=device, device_id_type=MESH)

    @pl.when(has_relay)
    def _():
        pl.semaphore_signal(barrier, inc=1, device_id=relay_dev, device_id_type=MESH)

    @pl.when(has_far)
    def _():
        pl.semaphore_signal(barrier, inc=1, device_id=far_dev, device_id_type=MESH)

    for p in range(len(PAIRS)):
        for k in range(3):
            band_copy(p, k).start()

    first = (shifts[0] == 1)
    occ1 = jnp.where(first, occupation[0], occupation[1])
    occ2 = jnp.where(first, occupation[1], occupation[0])
    pick = jnp.where(first, 0, 1)
    pair_c[:, :size] = coupling[pick]
    pair_c[:, size:] = coupling[1 - pick]

    @pl.when(jnp.logical_not(has_far))
    def _():
        far[...] = jnp.zeros_like(far)

    own_weight = jnp.where(xb == 0, occ1, 1.0 + occ1)
    other_weight = jnp.where(xb == 0, 1.0 + occ1, occ1)
    near_weight = jnp.where(yb == 0, 1.0 + occ2, occ2)
    far_weight = jnp.where(yb == 0, occ2, 1.0 + occ2)

    for slot in range(2):
        for part in range(2):
            base_copy(slot, part).wait()
        rows = pl.ds(slot * size, size)
        own[0, rows] = base[rows].astype(jnp.bfloat16)
        if slot == 0:
            peers = 3 + has_relay.astype(jnp.int32) + has_far.astype(jnp.int32)
            pl.semaphore_wait(barrier, peers)

        @pl.loop(slot * per_block, (slot + 1) * per_block)
        def _(c):
            own_copy(0, c).start()

    for p in range(len(PAIRS)):
        for k in range(3):
            band_copy(p, k).wait()
        band[p, pl.ds(size, size), pl.ds(0, size)] = -band[p, pl.ds(0, size), pl.ds(size, size)]

    def send_mixture(t, c, other):
        rows = rows_of(c)
        mixed = own_weight * own[t, rows].astype(jnp.float32)
        mixed = mixed + other_weight * other[t, rows].astype(jnp.float32)
        mix_out[t, rows] = mixed.astype(jnp.bfloat16)
        mix_copy(t, c).start()

    def near_step(t, c):
        own_copy(t, c).wait_recv()

        @pl.when(has_relay)
        def _():
            relay_copy(t, c).start()

        @pl.when(xb == yb)
        def _():
            send_mixture(t, c, near)

    def far_step(t, c):
        @pl.when(has_far)
        def _():
            relay_copy(t, c).wait_recv()

        @pl.when(xb != yb)
        def _():
            send_mixture(t, c, far)

        rows = rows_of(c)
        mixed = near_weight * near[t, rows].astype(jnp.float32)
        mixed = mixed + far_weight * far[t, rows].astype(jnp.float32)
        mode2[rows] = mixed.astype(jnp.bfloat16)

    def step(t, c):
        near_step(t, c)
        far_step(t, c - 1)

    def widen(t, source):
        wide[t, source, size:, :size] = -wide[t, source, :size, size:]
        wide[t, source, size:, size:] = wide[t, source, :size, :size]

    def scatter(t, slot):
        @pl.loop(slot * per_block, (slot + 1) * per_block)
        def _(c):
            mix_copy(t, c).wait_recv()

        rows = pl.ds(slot * size, size)
        for part in range(2):
            cols = pl.ds(part * size, size)
            half[:size, cols] = dot_nt(mix_in[t, rows, cols], pair_c[:, :size]).astype(jnp.bfloat16)
            half[size:, cols] = dot_nt(mode2[rows, cols], pair_c[:, size:]).astype(jnp.bfloat16)
        wide[t, 2 * slot, :size] = dot(pair_c[...], half[...]).astype(jnp.bfloat16)
        wide_copy(t, slot).start()
        widen(t, 2 * slot)

    def receive(t, slot):
        wide_copy(t, slot).wait_recv()
        widen(t, 2 * slot + 1)

    def pair(t, p):
        slot, source = PAIRS[p]
        rows = pl.ds(slot * size, size)
        start = base if p < 2 else total

        left[...] = dot(band[p, :size], wide[t, source]).astype(jnp.bfloat16)
        total[rows] = start[rows] + dot_nt(left[...], band[p])

    def out_copy(slot, part):
        return pltpu.make_async_copy(
            total.at[pl.ds(slot * size, size), pl.ds(part * size, size)],
            lesser.at[0, block_at(slot), part],
            out_sem.at[slot, part],
        )

    def finish(t, slot):
        if t == ITERS - 1:
            for part in range(2):
                out_copy(slot, part).start()
            return

        @pl.loop(slot * per_block, (slot + 1) * per_block)
        def _(c):
            own[t + 1, rows_of(c)] = total[rows_of(c)].astype(jnp.bfloat16)
            own_copy(t + 1, c).start()

    for t in range(ITERS):
        near_step(t, 0)
        lag = min(per_block + 3, steps)

        @pl.loop(1, lag)
        def _(c):
            step(t, c)

        scatter(t, 0)
        for p in range(4):
            if lag + p < steps:
                step(t, lag + p)
            if p == 2:
                receive(t, 0)
            pair(t, p)
        if lag + 4 < steps:
            @pl.loop(lag + 4, steps)
            def _(c):
                step(t, c)
        far_step(t, steps - 1)
        scatter(t, 1)
        pair(t, 4)
        receive(t, 1)
        pair(t, 5)
        finish(t, 0)
        pair(t, 6)
        finish(t, 1)

    for slot in range(2):
        for part in range(2):
            out_copy(slot, part).wait()
    for t in range(ITERS):
        for slot in range(2):
            wide_copy(t, slot).wait_send()

        @pl.loop(0, steps)
        def _(c):
            own_copy(t, c).wait_send()
            mix_copy(t, c).wait_send()

            @pl.when(has_relay)
            def _():
                relay_copy(t, c).wait_send()


def shards(energies, retarded, ballistic, coupling, occupation, shifts):
    count, blocks, _, size, _ = ballistic.shape
    assert count == 1 and blocks == 2 and energies % 4 == 0
    assert lax.axis_size("slab") == 2 and size % ROWS == 0
    width = 2 * size
    steps = 2 * size // ROWS
    blob = pltpu.VMEM((ITERS, 2 * size, width), jnp.bfloat16)
    flags = pltpu.SemaphoreType.DMA((ITERS, steps))
    pairs = len(PAIRS)
    flops = 2 * ITERS * (4 * pairs + 8) * width * width * size
    return pl.pallas_call(
        functools.partial(kernel, size, energies=energies),
        out_shape=jax.ShapeDtypeStruct(ballistic.shape, jnp.float32),
        in_specs=[
            pl.BlockSpec(memory_space=pl.ANY),
            pl.BlockSpec(memory_space=pl.ANY),
            pl.BlockSpec(memory_space=pltpu.VMEM),
            pl.BlockSpec(memory_space=pltpu.SMEM),
            pl.BlockSpec(memory_space=pltpu.SMEM),
        ],
        out_specs=pl.BlockSpec(memory_space=pl.ANY),
        scratch_shapes=[
            pltpu.VMEM((2 * size, width), jnp.float32),
            pltpu.VMEM((2 * size, width), jnp.float32),
            blob,
            blob,
            blob,
            blob,
            blob,
            pltpu.VMEM((2 * size, width), jnp.bfloat16),
            pltpu.VMEM((pairs, width, width), jnp.bfloat16),
            pltpu.VMEM((ITERS, 4, width, width), jnp.bfloat16),
            pltpu.VMEM((width, width), jnp.bfloat16),
            pltpu.VMEM((size, width), jnp.bfloat16),
            pltpu.VMEM((size, width), jnp.bfloat16),
            pltpu.SemaphoreType.DMA((2, 2)),
            pltpu.SemaphoreType.DMA((pairs, 3)),
            flags,
            flags,
            flags,
            pltpu.SemaphoreType.DMA((ITERS, 2)),
            flags,
            flags,
            flags,
            pltpu.SemaphoreType.DMA((ITERS, 2)),
            pltpu.SemaphoreType.DMA((2, 2)),
        ],
        cost_estimate=pl.CostEstimate(
            flops=flops, bytes_accessed=retarded.size * 2 + ballistic.size * 8, transcendentals=0
        ),
        compiler_params=pltpu.CompilerParams(
            collective_id=0, has_side_effects=True, vmem_limit_bytes=56 * 1024 * 1024
        ),
    )(retarded, ballistic, coupling, occupation, shifts)


def solution(mesh):
    return jax.shard_map(
        functools.partial(shards, mesh.shape["energy"]),
        mesh=mesh,
        in_specs=(
            P("energy", "slab", None, None, None, None),
            P("energy", "slab", None, None, None),
            P(),
            P(),
            P(),
        ),
        out_specs=P("energy", "slab", None, None, None),
        check_vma=False,
    )
```

```python
import functools

import jax
import jax.numpy as jnp
from jax import lax
from jax.experimental import pallas as pl
from jax.experimental.pallas import tpu as pltpu
from jax.sharding import PartitionSpec as P

ITERS = 2
ROWS = 64
MESH = pl.DeviceIdType.MESH

PAIRS = ((0, 0), (1, 0), (0, 1), (1, 1), (0, 2), (0, 3), (1, 2))


def dot(a, b):
    return jnp.dot(a, b, preferred_element_type=jnp.float32)


def kernel(
    size, retarded, ballistic, coupling, occupation, shifts, lesser,
    base, total, own, near, far, mix_out, mix_in, mode2, band, turned, wide, half, left, pair_c, turned_c,
    base_sem, band_sem, own_send, relay_send, mix_send, wide_send,
    near_recv, far_recv, mix_recv, wide_recv, out_sem, energies,
):
    width = 2 * size
    per_block = size // ROWS
    steps = 2 * per_block
    e = lax.axis_index("energy")
    s = lax.axis_index("slab")
    xb = e % 2
    yb = (e // 2) % 2
    d = 1 - 2 * yb
    near_dev = (e + 2 * d, s)
    relay_dev = (e + 4 * d, s)
    far_dev = (e - 4 * d, s)
    mate_dev = (e + 1 - 2 * xb, s)
    slab_dev = (e, 1 - s)
    has_relay = jnp.logical_and(e + 4 * d >= 0, e + 4 * d < energies)
    has_far = jnp.logical_and(e - 4 * d >= 0, e - 4 * d < energies)

    def block_at(slot):
        return (1 - slot) * (1 - 2 * s) + s

    def offset_at(slot, source):
        here = 2 * s + block_at(slot)
        if source % 2 == 0:
            there = 2 * s + block_at(source // 2)
        else:
            a = 1 - source // 2
            there = 2 * (1 - s) + a * (2 * s - 1) + 1 - s
        return there - here + 2

    def base_copy(slot, part):
        return pltpu.make_async_copy(
            ballistic.at[0, block_at(slot), part],
            base.at[pl.ds(slot * size, size), pl.ds(part * size, size)],
            base_sem.at[slot, part],
        )

    def band_copy(p, part):
        slot, source = PAIRS[p]
        return pltpu.make_async_copy(
            retarded.at[0, block_at(slot), offset_at(slot, source), part],
            band.at[p, :, pl.ds(part * size, size)],
            band_sem.at[p, part],
        )

    def prepare(p):
        for part in range(2):
            band_copy(p, part).wait()
        real = band[p, :, :size].T
        imag = band[p, :, size:].T
        turned[p, :size, :size] = real
        turned[p, size:, size:] = real
        turned[p, size:, :size] = imag
        turned[p, :size, size:] = -imag

    def rows_of(c):
        return pl.ds(pl.multiple_of(c * ROWS, ROWS), ROWS)

    def remote(src, dst, send, recv, device):
        return pltpu.make_async_remote_copy(
            src_ref=src, dst_ref=dst, send_sem=send, recv_sem=recv,
            device_id=device, device_id_type=MESH,
        )

    def own_copy(t, c):
        return remote(
            own.at[t, rows_of(c)], near.at[t, rows_of(c)],
            own_send.at[t, c], near_recv.at[t, c], near_dev,
        )

    def relay_copy(t, c):
        return remote(
            near.at[t, rows_of(c)], far.at[t, rows_of(c)],
            relay_send.at[t, c], far_recv.at[t, c], relay_dev,
        )

    def mix_copy(t, c):
        return remote(
            mix_out.at[t, rows_of(c)], mix_in.at[t, rows_of(c)],
            mix_send.at[t, c], mix_recv.at[t, c], mate_dev,
        )

    def wide_copy(t, slot):
        return remote(
            wide.at[t, 2 * slot, pl.ds(0, size)], wide.at[t, 2 * slot + 1, pl.ds(0, size)],
            wide_send.at[t, slot], wide_recv.at[t, slot], slab_dev,
        )

    for slot in range(2):
        for part in range(2):
            base_copy(slot, part).start()

    barrier = pltpu.get_barrier_semaphore()
    for device in (near_dev, mate_dev, slab_dev):
        pl.semaphore_signal(barrier, inc=1, device_id=device, device_id_type=MESH)

    @pl.when(has_relay)
    def _():
        pl.semaphore_signal(barrier, inc=1, device_id=relay_dev, device_id_type=MESH)

    @pl.when(has_far)
    def _():
        pl.semaphore_signal(barrier, inc=1, device_id=far_dev, device_id_type=MESH)

    for p in range(len(PAIRS)):
        for part in range(2):
            band_copy(p, part).start()

    first = (shifts[0] == 1)
    occ1 = jnp.where(first, occupation[0], occupation[1])
    occ2 = jnp.where(first, occupation[1], occupation[0])
    pick = jnp.where(first, 0, 1)
    pair_c[:, :size] = coupling[pick]
    pair_c[:, size:] = coupling[1 - pick]

    @pl.when(jnp.logical_not(has_far))
    def _():
        far[...] = jnp.zeros_like(far)

    own_weight = jnp.where(xb == 0, occ1, 1.0 + occ1)
    other_weight = jnp.where(xb == 0, 1.0 + occ1, occ1)
    near_weight = jnp.where(yb == 0, 1.0 + occ2, occ2)
    far_weight = jnp.where(yb == 0, occ2, 1.0 + occ2)

    for slot in range(2):
        for part in range(2):
            base_copy(slot, part).wait()
        rows = pl.ds(slot * size, size)
        own[0, rows] = base[rows].astype(jnp.bfloat16)
        if slot == 0:
            peers = 3 + has_relay.astype(jnp.int32) + has_far.astype(jnp.int32)
            pl.semaphore_wait(barrier, peers)

        @pl.loop(slot * per_block, (slot + 1) * per_block)
        def _(c):
            own_copy(0, c).start()

    for mode in range(2):
        turned_c[mode] = pair_c[:, mode * size : (mode + 1) * size].T

    def send_mixture(t, c, other):
        rows = rows_of(c)
        mixed = own_weight * own[t, rows].astype(jnp.float32)
        mixed = mixed + other_weight * other[t, rows].astype(jnp.float32)
        mix_out[t, rows] = mixed.astype(jnp.bfloat16)
        mix_copy(t, c).start()

    def near_step(t, c):
        own_copy(t, c).wait_recv()

        @pl.when(has_relay)
        def _():
            relay_copy(t, c).start()

        @pl.when(xb == yb)
        def _():
            send_mixture(t, c, near)

    def far_step(t, c):
        @pl.when(has_far)
        def _():
            relay_copy(t, c).wait_recv()

        @pl.when(xb != yb)
        def _():
            send_mixture(t, c, far)

        rows = rows_of(c)
        mixed = near_weight * near[t, rows].astype(jnp.float32)
        mixed = mixed + far_weight * far[t, rows].astype(jnp.float32)
        mode2[rows] = mixed.astype(jnp.bfloat16)

    def step(t, c):
        near_step(t, c)
        far_step(t, c - 1)

    def widen(t, source):
        wide[t, source, size:, :size] = -wide[t, source, :size, size:]
        wide[t, source, size:, size:] = wide[t, source, :size, :size]

    def scatter(t, slot):
        @pl.loop(slot * per_block, (slot + 1) * per_block)
        def _(c):
            mix_copy(t, c).wait_recv()

        rows = pl.ds(slot * size, size)
        for part in range(2):
            cols = pl.ds(part * size, size)
            half[:size, cols] = dot(mix_in[t, rows, cols], turned_c[0]).astype(jnp.bfloat16)
            half[size:, cols] = dot(mode2[rows, cols], turned_c[1]).astype(jnp.bfloat16)
        wide[t, 2 * slot, :size] = dot(pair_c[...], half[...]).astype(jnp.bfloat16)
        wide_copy(t, slot).start()
        widen(t, 2 * slot)

    def receive(t, slot):
        wide_copy(t, slot).wait_recv()
        widen(t, 2 * slot + 1)

    def pair(t, p):
        slot, source = PAIRS[p]
        rows = pl.ds(slot * size, size)
        start = base if p < 2 else total

        left[...] = dot(band[p], wide[t, source]).astype(jnp.bfloat16)
        total[rows] = start[rows] + dot(left[...], turned[p])

    def out_copy(slot, part):
        return pltpu.make_async_copy(
            total.at[pl.ds(slot * size, size), pl.ds(part * size, size)],
            lesser.at[0, block_at(slot), part],
            out_sem.at[slot, part],
        )

    def finish(t, slot):
        if t == ITERS - 1:
            for part in range(2):
                out_copy(slot, part).start()
            return

        @pl.loop(slot * per_block, (slot + 1) * per_block)
        def _(c):
            own[t + 1, rows_of(c)] = total[rows_of(c)].astype(jnp.bfloat16)
            own_copy(t + 1, c).start()

    for t in range(ITERS):
        near_step(t, 0)
        lag = min(per_block + 3, steps)

        ready = 1
        if t == 0:
            for p in range(len(PAIRS)):
                prepare(p)
                if ready < lag:
                    step(t, ready)
                    ready += 1

        @pl.loop(ready, lag)
        def _(c):
            step(t, c)

        scatter(t, 0)
        for p in range(4):
            if lag + p < steps:
                step(t, lag + p)
            if p == 2:
                receive(t, 0)
            pair(t, p)
        if lag + 4 < steps:
            @pl.loop(lag + 4, steps)
            def _(c):
                step(t, c)
        far_step(t, steps - 1)
        scatter(t, 1)
        pair(t, 4)
        receive(t, 1)
        pair(t, 5)
        finish(t, 0)
        pair(t, 6)
        finish(t, 1)

    for slot in range(2):
        for part in range(2):
            out_copy(slot, part).wait()
    for t in range(ITERS):
        for slot in range(2):
            wide_copy(t, slot).wait_send()

        @pl.loop(0, steps)
        def _(c):
            own_copy(t, c).wait_send()
            mix_copy(t, c).wait_send()

            @pl.when(has_relay)
            def _():
                relay_copy(t, c).wait_send()


def shards(energies, retarded, ballistic, coupling, occupation, shifts):
    count, blocks, _, size, _ = ballistic.shape
    assert count == 1 and blocks == 2 and energies % 4 == 0
    assert lax.axis_size("slab") == 2 and size % ROWS == 0
    width = 2 * size
    steps = 2 * size // ROWS
    blob = pltpu.VMEM((ITERS, 2 * size, width), jnp.bfloat16)
    flags = pltpu.SemaphoreType.DMA((ITERS, steps))
    pairs = len(PAIRS)
    flops = 2 * ITERS * (4 * pairs + 8) * width * width * size
    return pl.pallas_call(
        functools.partial(kernel, size, energies=energies),
        out_shape=jax.ShapeDtypeStruct(ballistic.shape, jnp.float32),
        in_specs=[
            pl.BlockSpec(memory_space=pl.ANY),
            pl.BlockSpec(memory_space=pl.ANY),
            pl.BlockSpec(memory_space=pltpu.VMEM),
            pl.BlockSpec(memory_space=pltpu.SMEM),
            pl.BlockSpec(memory_space=pltpu.SMEM),
        ],
        out_specs=pl.BlockSpec(memory_space=pl.ANY),
        scratch_shapes=[
            pltpu.VMEM((2 * size, width), jnp.float32),
            pltpu.VMEM((2 * size, width), jnp.float32),
            blob,
            blob,
            blob,
            blob,
            blob,
            pltpu.VMEM((2 * size, width), jnp.bfloat16),
            pltpu.VMEM((pairs, size, width), jnp.bfloat16),
            pltpu.VMEM((pairs, width, width), jnp.bfloat16),
            pltpu.VMEM((ITERS, 4, width, width), jnp.bfloat16),
            pltpu.VMEM((width, width), jnp.bfloat16),
            pltpu.VMEM((size, width), jnp.bfloat16),
            pltpu.VMEM((size, width), jnp.bfloat16),
            pltpu.VMEM((2, size, size), jnp.bfloat16),
            pltpu.SemaphoreType.DMA((2, 2)),
            pltpu.SemaphoreType.DMA((pairs, 2)),
            flags,
            flags,
            flags,
            pltpu.SemaphoreType.DMA((ITERS, 2)),
            flags,
            flags,
            flags,
            pltpu.SemaphoreType.DMA((ITERS, 2)),
            pltpu.SemaphoreType.DMA((2, 2)),
        ],
        cost_estimate=pl.CostEstimate(
            flops=flops, bytes_accessed=retarded.size * 2 + ballistic.size * 8, transcendentals=0
        ),
        compiler_params=pltpu.CompilerParams(
            collective_id=0, has_side_effects=True, vmem_limit_bytes=56 * 1024 * 1024
        ),
    )(retarded, ballistic, coupling, occupation, shifts)


def solution(mesh):
    return jax.shard_map(
        functools.partial(shards, mesh.shape["energy"]),
        mesh=mesh,
        in_specs=(
            P("energy", "slab", None, None, None, None),
            P("energy", "slab", None, None, None),
            P(),
            P(),
            P(),
        ),
        out_specs=P("energy", "slab", None, None, None),
        check_vma=False,
    )
```

```python
import functools

import jax
import jax.numpy as jnp
from jax import lax
from jax.experimental import pallas as pl
from jax.experimental.pallas import tpu as pltpu
from jax.sharding import PartitionSpec as P

ITERS = 2
ROWS = 32
AHEAD = 6
MESH = pl.DeviceIdType.MESH

PAIRS = ((0, 0), (1, 0), (0, 1), (1, 1), (0, 2), (0, 3), (1, 2))


def dot(a, b):
    return jnp.dot(a, b, preferred_element_type=jnp.float32)


def dot_nt(a, b):
    return lax.dot_general(a, b, (((1,), (1,)), ((), ())), preferred_element_type=jnp.float32)


def kernel(
    size, retarded, ballistic, coupling, occupation, shifts, lesser,
    base, total, own, near, far, mix_out, mix_in, mode2, band, wide, half, left, pair_c,
    base_sem, band_sem, own_send, relay_send, mix_send, wide_send,
    near_recv, far_recv, mix_recv, wide_recv, out_sem, energies,
):
    width = 2 * size
    per_block = size // ROWS
    steps = 2 * per_block
    e = lax.axis_index("energy")
    s = lax.axis_index("slab")
    xb = e % 2
    yb = (e // 2) % 2
    d = 1 - 2 * yb
    near_dev = (e + 2 * d, s)
    relay_dev = (e + 4 * d, s)
    far_dev = (e - 4 * d, s)
    mate_dev = (e + 1 - 2 * xb, s)
    slab_dev = (e, 1 - s)
    has_relay = jnp.logical_and(e + 4 * d >= 0, e + 4 * d < energies)
    has_far = jnp.logical_and(e - 4 * d >= 0, e - 4 * d < energies)

    def block_at(slot):
        return (1 - slot) * (1 - 2 * s) + s

    def offset_at(slot, source):
        here = 2 * s + block_at(slot)
        if source % 2 == 0:
            there = 2 * s + block_at(source // 2)
        else:
            a = 1 - source // 2
            there = 2 * (1 - s) + a * (2 * s - 1) + 1 - s
        return there - here + 2

    def base_copy(slot, part):
        return pltpu.make_async_copy(
            ballistic.at[0, block_at(slot), part],
            base.at[pl.ds(slot * size, size), pl.ds(part * size, size)],
            base_sem.at[slot, part],
        )

    def band_copy(p, k):
        slot, source = PAIRS[p]
        part = (0, 1, 0)[k]
        row, col = ((0, 0), (0, 1), (1, 1))[k]
        return pltpu.make_async_copy(
            retarded.at[0, block_at(slot), offset_at(slot, source), part],
            band.at[p, pl.ds(row * size, size), pl.ds(col * size, size)],
            band_sem.at[p, k],
        )

    def rows_of(c):
        return pl.ds(pl.multiple_of(c * ROWS, ROWS), ROWS)

    def remote(src, dst, send, recv, device):
        return pltpu.make_async_remote_copy(
            src_ref=src, dst_ref=dst, send_sem=send, recv_sem=recv,
            device_id=device, device_id_type=MESH,
        )

    def own_copy(t, c):
        return remote(
            own.at[t, rows_of(c)], near.at[t, rows_of(c)],
            own_send.at[t, c], near_recv.at[t, c], near_dev,
        )

    def relay_copy(t, c):
        return remote(
            near.at[t, rows_of(c)], far.at[t, rows_of(c)],
            relay_send.at[t, c], far_recv.at[t, c], relay_dev,
        )

    def mix_copy(t, c):
        return remote(
            mix_out.at[t, rows_of(c)], mix_in.at[t, rows_of(c)],
            mix_send.at[t, c], mix_recv.at[t, c], mate_dev,
        )

    def wide_copy(t, slot):
        return remote(
            wide.at[t, 2 * slot, pl.ds(0, size)], wide.at[t, 2 * slot + 1, pl.ds(0, size)],
            wide_send.at[t, slot], wide_recv.at[t, slot], slab_dev,
        )

    for slot in range(2):
        for part in range(2):
            base_copy(slot, part).start()

    barrier = pltpu.get_barrier_semaphore()
    for device in (near_dev, mate_dev, slab_dev):
        pl.semaphore_signal(barrier, inc=1, device_id=device, device_id_type=MESH)

    @pl.when(has_relay)
    def _():
        pl.semaphore_signal(barrier, inc=1, device_id=relay_dev, device_id_type=MESH)

    @pl.when(has_far)
    def _():
        pl.semaphore_signal(barrier, inc=1, device_id=far_dev, device_id_type=MESH)

    for p in range(len(PAIRS)):
        for k in range(3):
            band_copy(p, k).start()

    first = (shifts[0] == 1)
    occ1 = jnp.where(first, occupation[0], occupation[1])
    occ2 = jnp.where(first, occupation[1], occupation[0])
    pick = jnp.where(first, 0, 1)
    pair_c[:, :size] = coupling[pick]
    pair_c[:, size:] = coupling[1 - pick]

    @pl.when(jnp.logical_not(has_far))
    def _():
        far[...] = jnp.zeros_like(far)

    own_weight = jnp.where(xb == 0, occ1, 1.0 + occ1)
    other_weight = jnp.where(xb == 0, 1.0 + occ1, occ1)
    near_weight = jnp.where(yb == 0, 1.0 + occ2, occ2)
    far_weight = jnp.where(yb == 0, occ2, 1.0 + occ2)

    for slot in range(2):
        for part in range(2):
            base_copy(slot, part).wait()
        rows = pl.ds(slot * size, size)
        own[0, rows] = base[rows].astype(jnp.bfloat16)
        if slot == 0:
            peers = 3 + has_relay.astype(jnp.int32) + has_far.astype(jnp.int32)
            pl.semaphore_wait(barrier, peers)

            @pl.loop(0, AHEAD)
            def _(c):
                own_copy(0, c).start()

    for p in range(len(PAIRS)):
        for k in range(3):
            band_copy(p, k).wait()
        band[p, pl.ds(size, size), pl.ds(0, size)] = -band[p, pl.ds(0, size), pl.ds(size, size)]

    def send_mixture(t, c, other):
        rows = rows_of(c)
        mixed = own_weight * own[t, rows].astype(jnp.float32)
        mixed = mixed + other_weight * other[t, rows].astype(jnp.float32)
        mix_out[t, rows] = mixed.astype(jnp.bfloat16)
        mix_copy(t, c).start()

    def near_step(t, c):
        own_copy(t, c).wait_recv()

        @pl.when(c + AHEAD < steps)
        def _():
            own_copy(t, c + AHEAD).start()

        @pl.when(has_relay)
        def _():
            relay_copy(t, c).start()

        @pl.when(xb == yb)
        def _():
            send_mixture(t, c, near)

    def far_step(t, c):
        @pl.when(has_far)
        def _():
            relay_copy(t, c).wait_recv()

        @pl.when(xb != yb)
        def _():
            send_mixture(t, c, far)

        rows = rows_of(c)
        mixed = near_weight * near[t, rows].astype(jnp.float32)
        mixed = mixed + far_weight * far[t, rows].astype(jnp.float32)
        mode2[rows] = mixed.astype(jnp.bfloat16)

    def step(t, c):
        near_step(t, c)
        far_step(t, c - 1)

    def widen(t, source):
        wide[t, source, size:, :size] = -wide[t, source, :size, size:]
        wide[t, source, size:, size:] = wide[t, source, :size, :size]

    def scatter(t, slot):
        rows = pl.ds(slot * size, size)
        for part in range(2):
            cols = pl.ds(part * size, size)
            half[size:, cols] = dot_nt(mode2[rows, cols], pair_c[:, size:]).astype(jnp.bfloat16)

        @pl.loop(slot * per_block, (slot + 1) * per_block)
        def _(c):
            mix_copy(t, c).wait_recv()

        for part in range(2):
            cols = pl.ds(part * size, size)
            half[:size, cols] = dot_nt(mix_in[t, rows, cols], pair_c[:, :size]).astype(jnp.bfloat16)
        wide[t, 2 * slot, :size] = dot(pair_c[...], half[...]).astype(jnp.bfloat16)
        wide_copy(t, slot).start()
        widen(t, 2 * slot)

    def receive(t, slot):
        wide_copy(t, slot).wait_recv()
        widen(t, 2 * slot + 1)

    def pair(t, p):
        slot, source = PAIRS[p]
        rows = pl.ds(slot * size, size)
        start = base if p < 2 else total

        left[...] = dot(band[p, :size], wide[t, source]).astype(jnp.bfloat16)
        total[rows] = start[rows] + dot_nt(left[...], band[p])

    def out_copy(slot, part):
        return pltpu.make_async_copy(
            total.at[pl.ds(slot * size, size), pl.ds(part * size, size)],
            lesser.at[0, block_at(slot), part],
            out_sem.at[slot, part],
        )

    def finish(t, slot):
        if t == ITERS - 1:
            for part in range(2):
                out_copy(slot, part).start()
            return

        rows = pl.ds(slot * size, size)
        own[t + 1, rows] = total[rows].astype(jnp.bfloat16)
        if slot == 0:
            @pl.loop(0, AHEAD)
            def _(c):
                own_copy(t + 1, c).start()

    for t in range(ITERS):
        near_step(t, 0)
        lag = (7 * steps) // 10

        @pl.loop(1, lag)
        def _(c):
            step(t, c)

        scatter(t, 0)
        for p in range(3):
            @pl.loop(lag + (steps - lag) * p // 3, lag + (steps - lag) * (p + 1) // 3)
            def _(c):
                step(t, c)

            if p == 2:
                far_step(t, steps - 1)
                receive(t, 0)
            pair(t, p)
        pair(t, 3)
        scatter(t, 1)
        pair(t, 4)
        receive(t, 1)
        pair(t, 5)
        finish(t, 0)
        pair(t, 6)
        finish(t, 1)

    for slot in range(2):
        for part in range(2):
            out_copy(slot, part).wait()
    for t in range(ITERS):
        for slot in range(2):
            wide_copy(t, slot).wait_send()

        @pl.loop(0, steps)
        def _(c):
            own_copy(t, c).wait_send()
            mix_copy(t, c).wait_send()

            @pl.when(has_relay)
            def _():
                relay_copy(t, c).wait_send()


def shards(energies, retarded, ballistic, coupling, occupation, shifts):
    count, blocks, _, size, _ = ballistic.shape
    assert count == 1 and blocks == 2 and energies % 4 == 0
    assert lax.axis_size("slab") == 2 and size % ROWS == 0
    width = 2 * size
    steps = 2 * size // ROWS
    blob = pltpu.VMEM((ITERS, 2 * size, width), jnp.bfloat16)
    flags = pltpu.SemaphoreType.DMA((ITERS, steps))
    pairs = len(PAIRS)
    flops = 2 * ITERS * (4 * pairs + 8) * width * width * size
    return pl.pallas_call(
        functools.partial(kernel, size, energies=energies),
        out_shape=jax.ShapeDtypeStruct(ballistic.shape, jnp.float32),
        in_specs=[
            pl.BlockSpec(memory_space=pl.ANY),
            pl.BlockSpec(memory_space=pl.ANY),
            pl.BlockSpec(memory_space=pltpu.VMEM),
            pl.BlockSpec(memory_space=pltpu.SMEM),
            pl.BlockSpec(memory_space=pltpu.SMEM),
        ],
        out_specs=pl.BlockSpec(memory_space=pl.ANY),
        scratch_shapes=[
            pltpu.VMEM((2 * size, width), jnp.float32),
            pltpu.VMEM((2 * size, width), jnp.float32),
            blob,
            blob,
            blob,
            blob,
            blob,
            pltpu.VMEM((2 * size, width), jnp.bfloat16),
            pltpu.VMEM((pairs, width, width), jnp.bfloat16),
            pltpu.VMEM((ITERS, 4, width, width), jnp.bfloat16),
            pltpu.VMEM((width, width), jnp.bfloat16),
            pltpu.VMEM((size, width), jnp.bfloat16),
            pltpu.VMEM((size, width), jnp.bfloat16),
            pltpu.SemaphoreType.DMA((2, 2)),
            pltpu.SemaphoreType.DMA((pairs, 3)),
            flags,
            flags,
            flags,
            pltpu.SemaphoreType.DMA((ITERS, 2)),
            flags,
            flags,
            flags,
            pltpu.SemaphoreType.DMA((ITERS, 2)),
            pltpu.SemaphoreType.DMA((2, 2)),
        ],
        cost_estimate=pl.CostEstimate(
            flops=flops, bytes_accessed=retarded.size * 2 + ballistic.size * 8, transcendentals=0
        ),
        compiler_params=pltpu.CompilerParams(
            collective_id=0, has_side_effects=True, vmem_limit_bytes=56 * 1024 * 1024
        ),
    )(retarded, ballistic, coupling, occupation, shifts)


def solution(mesh):
    return jax.shard_map(
        functools.partial(shards, mesh.shape["energy"]),
        mesh=mesh,
        in_specs=(
            P("energy", "slab", None, None, None, None),
            P("energy", "slab", None, None, None),
            P(),
            P(),
            P(),
        ),
        out_specs=P("energy", "slab", None, None, None),
        check_vma=False,
    )
```

```python
import functools

import jax
import jax.numpy as jnp
from jax import lax
from jax.experimental import pallas as pl
from jax.experimental.pallas import tpu as pltpu
from jax.sharding import PartitionSpec as P

ITERS = 2
ROWS = 64
MESH = pl.DeviceIdType.MESH

PAIRS = ((0, 0), (1, 0), (0, 1), (1, 1), (0, 2), (0, 3), (1, 2))


def dot(a, b):
    return jnp.dot(a, b, preferred_element_type=jnp.float32)


def dot_nt(a, b):
    return lax.dot_general(a, b, (((1,), (1,)), ((), ())), preferred_element_type=jnp.float32)


def kernel(
    size, retarded, ballistic, coupling, occupation, shifts, lesser,
    base, total, own, near, far, mix_out, mix_in, mode2, band, wide, half, left, pair_c,
    base_sem, band_sem, own_send, relay_send, mix_send, wide_send,
    near_recv, far_recv, mix_recv, wide_recv, out_sem, energies,
):
    width = 2 * size
    per_block = size // ROWS
    steps = 2 * per_block
    e = lax.axis_index("energy")
    s = lax.axis_index("slab")
    xb = e % 2
    yb = (e // 2) % 2
    d = 1 - 2 * yb
    near_dev = (e + 2 * d, s)
    relay_dev = (e + 4 * d, s)
    far_dev = (e - 4 * d, s)
    mate_dev = (e + 1 - 2 * xb, s)
    slab_dev = (e, 1 - s)
    has_relay = jnp.logical_and(e + 4 * d >= 0, e + 4 * d < energies)
    has_far = jnp.logical_and(e - 4 * d >= 0, e - 4 * d < energies)

    def block_at(slot):
        return (1 - slot) * (1 - 2 * s) + s

    def offset_at(slot, source):
        here = 2 * s + block_at(slot)
        if source % 2 == 0:
            there = 2 * s + block_at(source // 2)
        else:
            a = 1 - source // 2
            there = 2 * (1 - s) + a * (2 * s - 1) + 1 - s
        return there - here + 2

    def base_copy(slot, part):
        return pltpu.make_async_copy(
            ballistic.at[0, block_at(slot), part],
            base.at[pl.ds(slot * size, size), pl.ds(part * size, size)],
            base_sem.at[slot, part],
        )

    def band_copy(p, k):
        slot, source = PAIRS[p]
        part = (0, 1, 0)[k]
        row, col = ((0, 0), (0, 1), (1, 1))[k]
        return pltpu.make_async_copy(
            retarded.at[0, block_at(slot), offset_at(slot, source), part],
            band.at[p, pl.ds(row * size, size), pl.ds(col * size, size)],
            band_sem.at[p, k],
        )

    def rows_of(c):
        return pl.ds(pl.multiple_of(c * ROWS, ROWS), ROWS)

    def remote(src, dst, send, recv, device):
        return pltpu.make_async_remote_copy(
            src_ref=src, dst_ref=dst, send_sem=send, recv_sem=recv,
            device_id=device, device_id_type=MESH,
        )

    def own_copy(t, c):
        return remote(
            own.at[t, rows_of(c)], near.at[t, rows_of(c)],
            own_send.at[t, c], near_recv.at[t, c], near_dev,
        )

    def relay_copy(t, c):
        return remote(
            near.at[t, rows_of(c)], far.at[t, rows_of(c)],
            relay_send.at[t, c], far_recv.at[t, c], relay_dev,
        )

    def mix_copy(t, c):
        return remote(
            mix_out.at[t, rows_of(c)], mix_in.at[t, rows_of(c)],
            mix_send.at[t, c], mix_recv.at[t, c], mate_dev,
        )

    def wide_copy(t, slot):
        return remote(
            wide.at[t, 2 * slot, pl.ds(0, size)], wide.at[t, 2 * slot + 1, pl.ds(0, size)],
            wide_send.at[t, slot], wide_recv.at[t, slot], slab_dev,
        )

    for slot in range(2):
        for part in range(2):
            base_copy(slot, part).start()

    barrier = pltpu.get_barrier_semaphore()
    for device in (near_dev, mate_dev, slab_dev):
        pl.semaphore_signal(barrier, inc=1, device_id=device, device_id_type=MESH)

    @pl.when(has_relay)
    def _():
        pl.semaphore_signal(barrier, inc=1, device_id=relay_dev, device_id_type=MESH)

    @pl.when(has_far)
    def _():
        pl.semaphore_signal(barrier, inc=1, device_id=far_dev, device_id_type=MESH)

    for p in range(len(PAIRS)):
        for k in range(3):
            band_copy(p, k).start()

    first = (shifts[0] == 1)
    occ1 = jnp.where(first, occupation[0], occupation[1])
    occ2 = jnp.where(first, occupation[1], occupation[0])
    pick = jnp.where(first, 0, 1)
    pair_c[:, :size] = coupling[pick]
    pair_c[:, size:] = coupling[1 - pick]

    @pl.when(jnp.logical_not(has_far))
    def _():
        far[...] = jnp.zeros_like(far)

    own_weight = jnp.where(xb == 0, occ1, 1.0 + occ1)
    other_weight = jnp.where(xb == 0, 1.0 + occ1, occ1)
    near_weight = jnp.where(yb == 0, 1.0 + occ2, occ2)
    far_weight = jnp.where(yb == 0, occ2, 1.0 + occ2)

    for slot in range(2):
        for part in range(2):
            base_copy(slot, part).wait()
        rows = pl.ds(slot * size, size)
        own[0, rows] = base[rows].astype(jnp.bfloat16)
        if slot == 0:
            peers = 3 + has_relay.astype(jnp.int32) + has_far.astype(jnp.int32)
            pl.semaphore_wait(barrier, peers)

        @pl.loop(slot * per_block, (slot + 1) * per_block)
        def _(c):
            own_copy(0, c).start()

    for p in range(len(PAIRS)):
        for k in range(3):
            band_copy(p, k).wait()
        band[p, pl.ds(size, size), pl.ds(0, size)] = -band[p, pl.ds(0, size), pl.ds(size, size)]

    def send_mixture(t, c, other):
        rows = rows_of(c)
        mixed = own_weight * own[t, rows].astype(jnp.float32)
        mixed = mixed + other_weight * other[t, rows].astype(jnp.float32)
        mix_out[t, rows] = mixed.astype(jnp.bfloat16)
        mix_copy(t, c).start()

    def near_step(t, c):
        own_copy(t, c).wait_recv()

        @pl.when(has_relay)
        def _():
            relay_copy(t, c).start()

        @pl.when(xb == yb)
        def _():
            send_mixture(t, c, near)

    def far_step(t, c):
        @pl.when(has_far)
        def _():
            relay_copy(t, c).wait_recv()

        @pl.when(xb != yb)
        def _():
            send_mixture(t, c, far)

        rows = rows_of(c)
        mixed = near_weight * near[t, rows].astype(jnp.float32)
        mixed = mixed + far_weight * far[t, rows].astype(jnp.float32)
        mode2[rows] = mixed.astype(jnp.bfloat16)

    def step(t, c):
        near_step(t, c)
        far_step(t, c - 1)

    def widen(t, source):
        wide[t, source, size:, :size] = -wide[t, source, :size, size:]
        wide[t, source, size:, size:] = wide[t, source, :size, :size]

    def scatter(t, slot):
        rows = pl.ds(slot * size, size)
        for part in range(2):
            cols = pl.ds(part * size, size)
            half[size:, cols] = dot_nt(mode2[rows, cols], pair_c[:, size:]).astype(jnp.bfloat16)

        @pl.loop(slot * per_block, (slot + 1) * per_block)
        def _(c):
            mix_copy(t, c).wait_recv()

        for part in range(2):
            cols = pl.ds(part * size, size)
            half[:size, cols] = dot_nt(mix_in[t, rows, cols], pair_c[:, :size]).astype(jnp.bfloat16)
        wide[t, 2 * slot, :size] = dot(pair_c[...], half[...]).astype(jnp.bfloat16)
        wide_copy(t, slot).start()
        widen(t, 2 * slot)

    def receive(t, slot):
        wide_copy(t, slot).wait_recv()
        widen(t, 2 * slot + 1)

    def pair(t, p):
        slot, source = PAIRS[p]
        rows = pl.ds(slot * size, size)
        start = base if p < 2 else total

        left[...] = dot(band[p, :size], wide[t, source]).astype(jnp.bfloat16)
        total[rows] = start[rows] + dot_nt(left[...], band[p])

    def out_copy(slot, part):
        return pltpu.make_async_copy(
            total.at[pl.ds(slot * size, size), pl.ds(part * size, size)],
            lesser.at[0, block_at(slot), part],
            out_sem.at[slot, part],
        )

    def finish(t, slot):
        if t == ITERS - 1:
            for part in range(2):
                out_copy(slot, part).start()
            return

        @pl.loop(slot * per_block, (slot + 1) * per_block)
        def _(c):
            own[t + 1, rows_of(c)] = total[rows_of(c)].astype(jnp.bfloat16)
            own_copy(t + 1, c).start()

    for t in range(ITERS):
        near_step(t, 0)
        lag = (3 * steps) // 4

        @pl.loop(1, lag)
        def _(c):
            step(t, c)

        scatter(t, 0)
        for p in range(3):
            @pl.loop(lag + (steps - lag) * p // 3, lag + (steps - lag) * (p + 1) // 3)
            def _(c):
                step(t, c)

            if p == 2:
                receive(t, 0)
            pair(t, p)
        far_step(t, steps - 1)
        pair(t, 3)
        scatter(t, 1)
        pair(t, 4)
        if t == ITERS - 1:
            pair(t, 6)
            finish(t, 1)
        receive(t, 1)
        pair(t, 5)
        finish(t, 0)
        if t < ITERS - 1:
            pair(t, 6)
            finish(t, 1)

    for slot in range(2):
        for part in range(2):
            out_copy(slot, part).wait()
    for t in range(ITERS):
        for slot in range(2):
            wide_copy(t, slot).wait_send()

        @pl.loop(0, steps)
        def _(c):
            own_copy(t, c).wait_send()
            mix_copy(t, c).wait_send()

            @pl.when(has_relay)
            def _():
                relay_copy(t, c).wait_send()


def shards(energies, retarded, ballistic, coupling, occupation, shifts):
    count, blocks, _, size, _ = ballistic.shape
    assert count == 1 and blocks == 2 and energies % 4 == 0
    assert lax.axis_size("slab") == 2 and size % ROWS == 0
    width = 2 * size
    steps = 2 * size // ROWS
    blob = pltpu.VMEM((ITERS, 2 * size, width), jnp.bfloat16)
    flags = pltpu.SemaphoreType.DMA((ITERS, steps))
    pairs = len(PAIRS)
    flops = 2 * ITERS * (4 * pairs + 8) * width * width * size
    return pl.pallas_call(
        functools.partial(kernel, size, energies=energies),
        out_shape=jax.ShapeDtypeStruct(ballistic.shape, jnp.float32),
        in_specs=[
            pl.BlockSpec(memory_space=pl.ANY),
            pl.BlockSpec(memory_space=pl.ANY),
            pl.BlockSpec(memory_space=pltpu.VMEM),
            pl.BlockSpec(memory_space=pltpu.SMEM),
            pl.BlockSpec(memory_space=pltpu.SMEM),
        ],
        out_specs=pl.BlockSpec(memory_space=pl.ANY),
        scratch_shapes=[
            pltpu.VMEM((2 * size, width), jnp.float32),
            pltpu.VMEM((2 * size, width), jnp.float32),
            blob,
            blob,
            blob,
            blob,
            blob,
            pltpu.VMEM((2 * size, width), jnp.bfloat16),
            pltpu.VMEM((pairs, width, width), jnp.bfloat16),
            pltpu.VMEM((ITERS, 4, width, width), jnp.bfloat16),
            pltpu.VMEM((width, width), jnp.bfloat16),
            pltpu.VMEM((size, width), jnp.bfloat16),
            pltpu.VMEM((size, width), jnp.bfloat16),
            pltpu.SemaphoreType.DMA((2, 2)),
            pltpu.SemaphoreType.DMA((pairs, 3)),
            flags,
            flags,
            flags,
            pltpu.SemaphoreType.DMA((ITERS, 2)),
            flags,
            flags,
            flags,
            pltpu.SemaphoreType.DMA((ITERS, 2)),
            pltpu.SemaphoreType.DMA((2, 2)),
        ],
        cost_estimate=pl.CostEstimate(
            flops=flops, bytes_accessed=retarded.size * 2 + ballistic.size * 8, transcendentals=0
        ),
        compiler_params=pltpu.CompilerParams(
            collective_id=0, has_side_effects=True, vmem_limit_bytes=56 * 1024 * 1024
        ),
    )(retarded, ballistic, coupling, occupation, shifts)


def solution(mesh):
    return jax.shard_map(
        functools.partial(shards, mesh.shape["energy"]),
        mesh=mesh,
        in_specs=(
            P("energy", "slab", None, None, None, None),
            P("energy", "slab", None, None, None),
            P(),
            P(),
            P(),
        ),
        out_specs=P("energy", "slab", None, None, None),
        check_vma=False,
    )
```
